128 devices in a mesh: pass: 16 (over x, y), query: 8 (over z, core).
Axes of the slice: x: 4, y: 4, z: 4, core: 2. Of those that a mesh axis runs over, the one named last changes fastest.
Arguments:
- query_q: bfloat16 [16384, 4096], P(('pass', 'query')), may hold values from -6 to 6
- query_k: bfloat16 [16384, 512], P(('pass', 'query')), may hold values from -6 to 6
- query_v: bfloat16 [16384, 512], P(('pass', 'query')), may hold values from -0.5 to 0.5
- query_out: bfloat16 [16384, 4096], P(('pass', 'query')), may hold values from -0.5 to 0.5
- query_dout: bfloat16 [16384, 4096], P(('pass', 'query')), may hold values from -6 to 6
- query_lse: float32 [32, 16384], P(None, ('pass', 'query')), may hold values from 7 to 9
- query_seg: int32 [16, 1024], P('pass'), may hold values from 0 to 3, never falling along the last dimension, each value on 1 to 512 neighbouring positions
- passage_q: bfloat16 [8192, 4096], P(('pass', 'query')), may hold values from -6 to 6
- passage_k: bfloat16 [8192, 512], P(('pass', 'query')), may hold values from -6 to 6
- passage_v: bfloat16 [8192, 512], P(('pass', 'query')), may hold values from -0.5 to 0.5
- passage_out: bfloat16 [8192, 4096], P(('pass', 'query')), may hold values from -0.5 to 0.5
- passage_dout: bfloat16 [8192, 4096], P(('pass', 'query')), may hold values from -6 to 6
- passage_lse: float32 [32, 8192], P(None, ('pass', 'query')), may hold values from 4.5 to 6.5
- passage_len: int32 [16], replicated, may hold values from 384 to 512, as said below
- reads: int32 [16, 8], replicated, may hold values from 0 to 15, as said below
Outputs:
- query_dq: bfloat16 [16384, 4096], P(('pass', 'query'))
- query_dk: bfloat16 [16384, 512], P(('pass', 'query'))
- query_dv: bfloat16 [16384, 512], P(('pass', 'query'))
- passage_dq: bfloat16 [8192, 4096], P(('pass', 'query'))
- passage_dk: bfloat16 [8192, 512], P(('pass', 'query'))
- passage_dv: bfloat16 [8192, 512], P(('pass', 'query'))
The draws below stay inside these ranges and needn't reach their ends.
Inputs may be any that keep to these rules, and one draw needn't show every extreme that they name: `passage_len`: some passage has exactly 512 live tokens and some exactly 384. `reads`: each row lists 8 different passages; every passage is listed by some block. `query_seg`: within each query block the document ids never fall; each document has 1 to 512 positions, one exactly 512.
All inputs are finite; a program needn't handle non-finite values.
Results may differ from the reference program's by a relative error of at most 0.018.
Values may be sent and summed in bfloat16 or wider, within the bound.
A program may use at most 192 MiB of HBM per device.

```python
import math
import jax
import jax.numpy as jnp
import numpy as np
from jax import lax

H = 32
KVH = 4
HD = 128
QTOK_DEV = 128
PMAX = 512
SEGS = 4
READS = 8
QLEN = 1024
QTOKENS = 16384
PTOKENS = 8192
N_PASS = 16
N_QUERY = 8


def draw_passage_len(key, part):
    key = jax.random.fold_in(key, 23)
    shortest = PMAX - PMAX // 4
    lengths = jax.random.randint(jax.random.fold_in(key, 1), (N_PASS,), shortest, PMAX + 1, dtype=jnp.int32)
    longest_at = jax.random.randint(jax.random.fold_in(key, 2), (), 0, N_PASS, dtype=jnp.int32)
    step_away = jax.random.randint(jax.random.fold_in(key, 3), (), 0, N_PASS - 1, dtype=jnp.int32)
    short_at = (longest_at + 1 + step_away) % N_PASS
    places = jnp.arange(N_PASS, dtype=jnp.int32)
    lengths = jnp.where(places == longest_at, PMAX, lengths)
    return jnp.where(places == short_at, shortest, lengths).astype(jnp.int32)


def draw_reads(key, part):
    key = jax.random.fold_in(key, 11)
    leading = jax.random.permutation(jax.random.fold_in(key, 1), N_PASS).astype(jnp.int32)
    row_base = jax.random.fold_in(key, 2)

    def one_row(row_index):
        row_key = jax.random.fold_in(row_base, row_index)
        others = jax.random.permutation(row_key, N_PASS - 1).astype(jnp.int32)[:READS - 1]
        return (leading[row_index] + 1 + others) % N_PASS
    remaining = jax.vmap(one_row)(jnp.arange(N_PASS, dtype=jnp.int32))
    return jnp.concatenate([leading[:, None], remaining], axis=1).astype(jnp.int32)


def level_of(own_key, dims, shards, smallest, top_value):
    def one(axis_at, blocks):
        heights = jax.random.uniform(jax.random.fold_in(jax.random.fold_in(own_key, 6), axis_at), (blocks,), jnp.float32, smallest / len(shards), top_value / len(shards))
        return jnp.repeat(jnp.exp(heights), dims[axis_at] // blocks).reshape((-1,) + (1,) * (len(dims) - axis_at - 1))

    level = one(*shards[0])
    for cut in shards[1:]:
        level = level * one(*cut)
    return level


def split_up(count, total, most, slope):
    portions = [(1 << 20) // math.isqrt(rank ** slope) + 1 for rank in range(2, count + 1)]
    spare, holding = total - most - (count - 1), [1] * (count - 1)
    while spare > 0:
        candidates = [i for i in range(count - 1) if holding[i] < most]
        whole, left = sum([portions[i] for i in candidates]), spare
        for i in candidates:
            addition = min(most - holding[i], max(1, left * portions[i] // whole), spare)
            holding[i] = holding[i] + addition
            spare = spare - addition
    return np.array([most] + holding)


def ragged_sizes(key, number_of, total, bound, lean):
    if number_of == 2:
        one = jax.random.randint(key, (), max(1, total - bound), min(bound, total - 1) + 1)
        return jnp.stack([one, total - one])
    tallies = jnp.asarray(split_up(number_of, total, bound, lean), jnp.int32)
    couples = (number_of - 1) // 2
    donor, sink = tallies[1:1 + 2 * couples:2], tallies[2:2 + 2 * couples:2]
    margin = jnp.minimum(donor - 1, bound - sink)
    passed = jax.random.randint(jax.random.fold_in(key, 1), (couples,), 0, 1 << 20) % (margin + 1)
    tallies = tallies.at[1:1 + 2 * couples:2].set(donor - passed).at[2:2 + 2 * couples:2].set(sink + passed)
    return tallies[jax.random.permutation(jax.random.fold_in(key, 2), number_of)]


def normal_values(rng, dims, scale, reach, shards=(), held_as=jnp.bfloat16):
    drawn = jax.random.normal(rng, dims, jnp.float32) * scale
    if len(shards) > 0:
        drawn = level_of(rng, dims, shards, -0.22, 0.18) * drawn
    return jnp.clip(drawn, min=-reach, max=reach).astype(held_as)


def setup_inputs(seed: int = 0) -> dict:
    splits = jax.random.split(jax.random.key(seed), 16)
    query_q = normal_values(splits[0], (QTOKENS, H * HD), 1.0, 6.0, ((0, 128),))
    query_k = normal_values(splits[1], (QTOKENS, KVH * HD), 1.0, 6.0, ((0, 128),))
    query_v = normal_values(splits[2], (QTOKENS, KVH * HD), 0.09, 0.5, ((0, 128),))
    query_out = normal_values(splits[3], (QTOKENS, H * HD), 0.09, 0.5, ((0, 128),))
    query_dout = normal_values(splits[4], (QTOKENS, H * HD), 1.0, 6.0, ((0, 128),))
    query_lse = jnp.clip(7.0 + 2.0 * jax.random.uniform(splits[5], (H, QTOKENS), jnp.float32) ** level_of(splits[5], (H, QTOKENS), ((1, 128),), -0.2, 0.2), 7.0, 9.0)
    query_seg = jax.vmap(lambda own: jnp.searchsorted(jnp.cumsum(ragged_sizes(own, SEGS, QLEN, QLEN // 2, 0)), jnp.arange(QLEN), side="right"))(jax.random.split(splits[6], N_PASS)).reshape((N_PASS, QLEN)).astype(jnp.int32)
    passage_q = normal_values(splits[7], (PTOKENS, H * HD), 1.0, 6.0, ((0, 128),))
    passage_k = normal_values(splits[8], (PTOKENS, KVH * HD), 1.0, 6.0, ((0, 128),))
    passage_v = normal_values(splits[9], (PTOKENS, KVH * HD), 0.09, 0.5, ((0, 128),))
    passage_out = normal_values(splits[10], (PTOKENS, H * HD), 0.09, 0.5, ((0, 128),))
    passage_dout = normal_values(splits[11], (PTOKENS, H * HD), 1.0, 6.0, ((0, 128),))
    passage_lse = jnp.clip(4.5 + 2.0 * jax.random.uniform(splits[12], (H, PTOKENS), jnp.float32) ** level_of(splits[12], (H, PTOKENS), ((1, 128),), -0.2, 0.2), 4.5, 6.5)
    passage_len = draw_passage_len(jax.random.fold_in(splits[15], 71), 0)
    reads = draw_reads(jax.random.fold_in(splits[15], 71), 0)
    return {"query_q": query_q, "query_k": query_k, "query_v": query_v, "query_out": query_out, "query_dout": query_dout, "query_lse": query_lse, "query_seg": query_seg, "passage_q": passage_q, "passage_k": passage_k, "passage_v": passage_v, "passage_out": passage_out, "passage_dout": passage_dout, "passage_lse": passage_lse, "passage_len": passage_len, "reads": reads}


def attend_back(queries, keys, values, out_grad, log_norm, deltas, visible):
    query_rows = queries.shape[0]
    key_rows = keys.shape[0]
    groups = H // KVH
    scaling = HD ** -0.5
    query_heads = queries.astype(jnp.float32).reshape(query_rows, KVH, groups, HD)
    grad_heads = out_grad.astype(jnp.float32).reshape(query_rows, KVH, groups, HD)
    key_heads = keys.astype(jnp.float32).reshape(key_rows, KVH, HD)
    value_heads = values.astype(jnp.float32).reshape(key_rows, KVH, HD)
    norm_heads = log_norm.reshape(KVH, groups, query_rows)
    delta_heads = deltas.reshape(KVH, groups, query_rows)
    scores = jnp.einsum('qkgd,tkd->kgqt', query_heads, key_heads) * scaling
    weights = jnp.where(visible, jnp.exp(scores - norm_heads[..., None]), 0.0)
    weight_grad = jnp.einsum('qkgd,tkd->kgqt', grad_heads, value_heads)
    score_grad = weights * (weight_grad - delta_heads[..., None])
    weights_low = lax.optimization_barrier(weights.astype(jnp.bfloat16)).astype(jnp.float32)
    score_low = lax.optimization_barrier(score_grad.astype(jnp.bfloat16)).astype(jnp.float32)
    value_grad = jnp.einsum('kgqt,qkgd->tkd', weights_low, grad_heads).reshape(key_rows, KVH * HD)
    key_grad = jnp.einsum('kgqt,qkgd->tkd', score_low, query_heads).reshape(key_rows, KVH * HD) * scaling
    query_grad = jnp.einsum('kgqt,tkd->qkgd', score_low, key_heads).reshape(query_rows, H * HD) * scaling
    return query_grad, key_grad, value_grad


def row_delta(out_grad, outputs):
    product = out_grad.astype(jnp.float32) * outputs.astype(jnp.float32)
    return jnp.sum(product.reshape(-1, H, HD), axis=2).T


def rounded(parts):
    return lax.optimization_barrier(parts.astype(jnp.bfloat16)).astype(jnp.float32)


def reference(query_q, query_k, query_v, query_out, query_dout, query_lse, query_seg, passage_q, passage_k, passage_v, passage_out, passage_dout, passage_lse, passage_len, reads):
    devices = N_PASS * N_QUERY
    kv_width = KVH * HD
    pair_width = 2 * kv_width
    passage_rows = PMAX // N_QUERY
    query_delta = row_delta(query_dout, query_out)
    passage_delta = row_delta(passage_dout, passage_out)
    query_pairs = jnp.concatenate([query_k, query_v], axis=1)
    passage_pairs = jnp.concatenate([passage_k, passage_v], axis=1).reshape(N_PASS, PMAX, pair_width)
    positions = jnp.arange(PMAX, dtype=jnp.int32)
    live = positions[None, :] < passage_len[:, None]

    def visit_device(totals, device):
        self_total, passage_total = totals
        block_index = device // N_QUERY
        row_index = device % N_QUERY
        own_queries = lax.dynamic_slice_in_dim(query_q, device * QTOK_DEV, QTOK_DEV, 0)
        own_grads = lax.dynamic_slice_in_dim(query_dout, device * QTOK_DEV, QTOK_DEV, 0)
        own_norm = lax.dynamic_slice_in_dim(query_lse, device * QTOK_DEV, QTOK_DEV, 1)
        own_delta = lax.dynamic_slice_in_dim(query_delta, device * QTOK_DEV, QTOK_DEV, 1)
        block_pairs = lax.dynamic_slice_in_dim(query_pairs, block_index * QLEN, QLEN, 0)
        segments = lax.dynamic_index_in_dim(query_seg, block_index, 0, keepdims=False)
        query_pos = row_index * QTOK_DEV + jnp.arange(QTOK_DEV, dtype=jnp.int32)
        key_pos = jnp.arange(QLEN, dtype=jnp.int32)
        own_segments = lax.dynamic_slice_in_dim(segments, row_index * QTOK_DEV, QTOK_DEV, 0)
        self_mask = (key_pos[None, :] <= query_pos[:, None]) & (segments[None, :] == own_segments[:, None])
        chosen = lax.dynamic_index_in_dim(reads, block_index, 0, keepdims=False)
        read_pairs = jnp.take(passage_pairs, chosen, axis=0).reshape(READS * PMAX, pair_width)
        read_live = jnp.take(live, chosen, axis=0).reshape(READS * PMAX)
        all_keys = jnp.concatenate([block_pairs, read_pairs], axis=0)
        visible = jnp.concatenate([self_mask, jnp.broadcast_to(read_live[None, :], (QTOK_DEV, READS * PMAX))], axis=1)
        query_grad, key_grad, value_grad = attend_back(own_queries, all_keys[:, :kv_width], all_keys[:, kv_width:], own_grads, own_norm, own_delta, visible)
        partials = rounded(jnp.concatenate([key_grad, value_grad], axis=1))
        current = lax.dynamic_slice_in_dim(self_total, block_index * QLEN, QLEN, 0)
        self_total = lax.dynamic_update_slice_in_dim(self_total, current + partials[:QLEN], block_index * QLEN, 0)
        passage_total = passage_total.at[chosen].add(partials[QLEN:].reshape(READS, PMAX, pair_width))
        local_queries = lax.dynamic_slice_in_dim(passage_q, device * passage_rows, passage_rows, 0)
        local_grads = lax.dynamic_slice_in_dim(passage_dout, device * passage_rows, passage_rows, 0)
        local_norm = lax.dynamic_slice_in_dim(passage_lse, device * passage_rows, passage_rows, 1)
        local_delta = lax.dynamic_slice_in_dim(passage_delta, device * passage_rows, passage_rows, 1)
        own_passage = lax.dynamic_index_in_dim(passage_pairs, block_index, 0, keepdims=False)
        own_live = lax.dynamic_index_in_dim(live, block_index, 0, keepdims=False)
        local_pos = row_index * passage_rows + jnp.arange(passage_rows, dtype=jnp.int32)
        local_live = lax.dynamic_slice_in_dim(own_live, row_index * passage_rows, passage_rows, 0)
        local_mask = (positions[None, :] <= local_pos[:, None]) & own_live[None, :] & local_live[:, None]
        local_q, local_k, local_v = attend_back(local_queries, own_passage[:, :kv_width], own_passage[:, kv_width:], local_grads, local_norm, local_delta, local_mask)
        local_part = rounded(jnp.concatenate([local_k, local_v], axis=1))
        passage_total = passage_total.at[block_index].add(local_part)
        return (self_total, passage_total), (query_grad.astype(jnp.bfloat16), local_q.astype(jnp.bfloat16))

    start_totals = (jnp.zeros((N_PASS * QLEN, pair_width), jnp.float32), jnp.zeros((N_PASS, PMAX, pair_width), jnp.float32))
    (self_total, passage_total), (query_rows_grad, passage_rows_grad) = lax.scan(visit_device, start_totals, jnp.arange(devices, dtype=jnp.int32))
    query_dq = query_rows_grad.reshape(-1, H * HD)
    query_dk = self_total[:, :kv_width].astype(jnp.bfloat16)
    query_dv = self_total[:, kv_width:].astype(jnp.bfloat16)
    passage_dq = passage_rows_grad.reshape(-1, H * HD)
    passage_sum = passage_total.reshape(-1, pair_width)
    passage_dk = passage_sum[:, :kv_width].astype(jnp.bfloat16)
    passage_dv = passage_sum[:, kv_width:].astype(jnp.bfloat16)
    return query_dq, query_dk, query_dv, passage_dq, passage_dk, passage_dv
```

```python
import functools
import math

import jax
import jax.numpy as jnp
from jax import lax
from jax.experimental import pallas as pl
from jax.experimental.pallas import tpu as pltpu
from jax.sharding import PartitionSpec as P

H = 32
KVH = 4
HD = 128
GROUP = H // KVH
WIDE = GROUP * HD
QROWS = 128
PROWS = 64
READS = 8
PASSAGES = 16
SCALE = HD ** (-0.5)
LOG2E = math.log2(math.e)
FOLD = SCALE * LOG2E
HIDDEN = -1e30
NT = (((1,), (1,)), ((), ()))
MESH = pl.DeviceIdType.MESH
f32 = jnp.float32
bf16 = jnp.bfloat16


def tile(keys, values, queries, grads, norm, delta, bias=None):
    scores = lax.dot_general(keys, queries, NT, preferred_element_type=f32)
    slopes = lax.dot_general(values, grads, NT, preferred_element_type=f32)
    power = scores * FOLD - norm
    if bias is not None:
        power = power + bias
    weight = jnp.exp2(power)
    score = (weight * (slopes - delta)).astype(bf16)
    weight = weight.astype(bf16)
    dv = jnp.dot(weight, grads, preferred_element_type=f32)
    dk = jnp.dot(score, queries, preferred_element_type=f32)
    dqt = jnp.dot(keys.T, score, preferred_element_type=f32)
    return dk, dv, dqt


def heads_down(ref, *lead):
    return jnp.concatenate([ref[(*lead, slice(None), pl.ds(h * HD, HD))] for h in range(GROUP)], 0)


def heads_along(stat, first):
    return jnp.concatenate([stat[first + h : first + h + 1, :] for h in range(GROUP)], 1)


def body(
    reads, lens,
    q, k, v, out, dout, lse, seg,
    pq, pk, pv, pout, pdout, plse,
    dq_o, dk_o, dv_o, pdq_o, pdk_o, pdv_o,
    out_v, dout_v, pout_v, pdout_v,
    stat, pstat, st, pst,
    qa, da, pqa, pda,
    shard, kv_a, kv_b, bkv, segc,
    dqt, acc_a, acc_b, acc_s, acc_l,
    dqs, pdqs,
    cs_a, cs_b, cr_a, cr_b, ps_a, ps_b, pr_a, pr_b,
    ls_s, ls_r, ss_s, ss_r, fin, fin_s,
    zs, zr, gs, gr, xs, xr, es, er, rs, rr, bs, br, lo,
):
    b = lax.axis_index("pass")
    r = lax.axis_index("query")
    X, Y, Z, K = b // 4, b % 4, r // 2, r % 2
    other = 1 - K

    def zdev(d):
        return (b, ((Z + d) % 4) * 2 + K)

    def pdev(dx, dy):
        return (((X + dx) % 4) * 4 + (Y + dy) % 4, r)

    core = (b, Z * 2 + other)
    plane = [(dx, dy) for dx in range(4) for dy in range(4) if (dx, dy) != (0, 0)]
    halves = (0, 1)
    kv_h, acc_h = (kv_a, kv_b), (acc_a, acc_b)
    cs_h, cr_h, ps_h, pr_h = (cs_a, cs_b), (cr_a, cr_b), (ps_a, ps_b), (pr_a, pr_b)
    pending = []

    def remote(src, dst, s, rcv, to):
        return pltpu.make_async_remote_copy(
            src_ref=src, dst_ref=dst, send_sem=s, recv_sem=rcv, device_id=to, device_id_type=MESH
        )

    def send(*args):
        c = remote(*args)
        c.start()
        pending.append(c)
        return c

    def cols(index, width):
        return pl.ds(pl.multiple_of(index * width, width), width)

    barrier = pltpu.get_barrier_semaphore()
    greet = [zdev(d) for d in (1, 2, 3)] + [pdev(*o) for o in plane] + [core]
    for to in greet:
        pl.semaphore_signal(barrier, inc=1, device_id=to, device_id_type=MESH)
    pl.semaphore_wait(barrier, len(greet))

    def z_out(kind, d, src, dst):
        return send(src, dst, zs.at[kind, d - 1], zr.at[kind, d - 1], zdev(d))

    zc = {}
    for d in (1, 3, 2):
        c = (Z + d) % 4
        zc[0, d] = z_out(0, d, pk.at[:, cols(c, HD)], shard.at[Z, :, 0:HD])
        zc[1, d] = z_out(1, d, pv.at[:, cols(c, HD)], shard.at[Z, :, HD : 2 * HD])
    mine = []

    def local(src, dst):
        c = pltpu.make_async_copy(src, dst, lo.at[len(mine)])
        c.start()
        mine.append(c)
        return c

    own = [
        local(pk.at[:, cols(Z, HD)], shard.at[Z, :, 0:HD]),
        local(pv.at[:, cols(Z, HD)], shard.at[Z, :, HD : 2 * HD]),
    ]
    own_b = [
        local(k.at[:, cols(Z, HD)], bkv.at[Z, K, :, 0:HD]),
        local(v.at[:, cols(Z, HD)], bkv.at[Z, K, :, HD : 2 * HD]),
    ]
    own_q = [
        local(q.at[:, cols(Z, WIDE)], qa.at[0]),
        local(dout.at[:, cols(Z, WIDE)], da.at[0]),
    ]
    own_p = [
        local(pq.at[:, cols(Z, WIDE)], pqa.at[0]),
        local(pdout.at[:, cols(Z, WIDE)], pda.at[0]),
    ]
    own_d = [local(out, out_v), local(dout, dout_v), local(pout, pout_v), local(pdout, pdout_v)]
    for d in (1, 3, 2):
        c = (Z + d) % 4
        zc[2, d] = z_out(2, d, k.at[:, cols(c, HD)], bkv.at[Z, K, :, 0:HD])
        zc[3, d] = z_out(3, d, v.at[:, cols(c, HD)], bkv.at[Z, K, :, HD : 2 * HD])
    for d in (1, 3, 2):
        c = (Z + d) % 4
        zc[4, d] = z_out(4, d, q.at[:, cols(c, WIDE)], qa.at[d])
        zc[5, d] = z_out(5, d, dout.at[:, cols(c, WIDE)], da.at[d])

    for c in own:
        c.wait()
    for d in (1, 3, 2):
        zc[0, d].wait_recv()
        zc[1, d].wait_recv()
    gather = {}
    for half in halves:
        src = shard.at[2 * half : 2 * half + 2]
        dst = kv_h[half].at[b, :, K]
        local(src, dst)
        for i, o in enumerate(plane):
            gather[half, o] = send(src, dst, gs.at[half, i], gr.at[half, i], pdev(*o))
    own_g = mine[-2:]

    for d in (1, 3, 2):
        c = (Z + d) % 4
        zc[6, d] = z_out(6, d, pq.at[:, cols(c, WIDE)], pqa.at[d])
        zc[7, d] = z_out(7, d, pdout.at[:, cols(c, WIDE)], pda.at[d])

    pstat[...] = jnp.zeros_like(pstat)
    for c in own_d:
        c.wait()

    def group_stats(c, _):
        stat[c, 0:GROUP, :] = lse[pl.ds(pl.multiple_of(c * GROUP, GROUP), GROUP), :] * LOG2E
        pstat[c, 0:GROUP, 0:PROWS] = plse[pl.ds(pl.multiple_of(c * GROUP, GROUP), GROUP), :] * LOG2E
        for h in range(GROUP):
            at = pl.ds(pl.multiple_of(c * WIDE + h * HD, HD), HD)
            prod = dout_v[:, at].astype(f32) * out_v[:, at].astype(f32)
            stat[c, GROUP + h : GROUP + h + 1, :] = jnp.sum(prod.T, axis=0, keepdims=True)
            prod = pdout_v[:, at].astype(f32) * pout_v[:, at].astype(f32)
            pstat[c, GROUP + h : GROUP + h + 1, 0:PROWS] = jnp.sum(prod.T, axis=0, keepdims=True)
        return 0

    lax.fori_loop(0, KVH, group_stats, 0)
    for d in (1, 3, 2):
        c = (Z + d) % 4
        zc[8, d] = z_out(8, d, stat.at[c], st.at[d])
        zc[9, d] = z_out(9, d, pstat.at[c], pst.at[d])
    st[0] = stat[Z]
    pst[0] = pstat[Z]

    for ref in (dqt, acc_a, acc_b, acc_s, acc_l):
        ref[...] = jnp.zeros_like(ref)
    for block in range(8):
        row = seg[:, block * 128 : (block + 1) * 128].astype(f32)
        segc[block * 128 : (block + 1) * 128, :] = jnp.broadcast_to(row, (128, 128)).T

    def self_chunk(slot):
        rb = ((Z - slot + 4) % 4) * 2 + K
        first = jnp.clip(rb - 4, 0, 3)
        start = pl.multiple_of(first * 128, 128)
        at = pl.ds(start, 640)
        key_pos = start + lax.broadcasted_iota(jnp.int32, (640, 128), 0)
        row_pos = rb * 128 + lax.broadcasted_iota(jnp.int32, (640, 128), 1)
        row_seg = seg[:, pl.ds(pl.multiple_of(rb * 128, 128), 128)].astype(f32)
        seen = (key_pos <= row_pos) & (segc[at, :] == row_seg)
        bias = jnp.where(seen, 0.0, HIDDEN)
        pairs = [bkv[(first + i) // 2, (first + i) % 2] for i in range(5)]
        pairs = jnp.concatenate(pairs, 0)
        dk, dv, part = tile(
            pairs[:, :HD], pairs[:, HD:], heads_down(qa, slot), heads_down(da, slot),
            heads_along(st[slot], 0), heads_along(st[slot], GROUP),
            jnp.concatenate([bias] * GROUP, 1),
        )
        dqt[slot] += part
        for i in range(5):
            zi, ki = (first + i) // 2, (first + i) % 2
            acc_s[zi, ki, :, :HD] += dk[i * 128 : (i + 1) * 128]
            acc_s[zi, ki, :, HD:] += dv[i * 128 : (i + 1) * 128]

    def cross(half, slot, j):
        p = reads[b, j]
        pairs = kv_h[half][p].reshape(256, 2 * HD)
        if half == 1:
            pos = 256 + lax.broadcasted_iota(jnp.int32, (256, 2 * HD), 0)
            pairs = jnp.where(pos < lens[p], pairs.astype(f32), 0.0).astype(bf16)
        dk, dv, part = tile(
            pairs[:, :HD], pairs[:, HD:], heads_down(qa, slot), heads_down(da, slot),
            heads_along(st[slot], 0), heads_along(st[slot], GROUP),
        )
        dqt[slot] += part
        acc = acc_h[half]
        acc[j, :, :, :, :HD] += dk.reshape(2, 2, 64, HD)
        acc[j, :, :, :, HD:] += dv.reshape(2, 2, 64, HD)

    def cross_all(half, slot):
        def one(j, _):
            cross(half, slot, j)
            return 0
        lax.fori_loop(0, READS, one, 0)

    for c in own_b + own_q:
        c.wait()
    for d in (1, 3, 2):
        zc[2, d].wait_recv()
        zc[3, d].wait_recv()
    fwd = {}

    def forward(half):
        for dx in range(4):
            for dy in range(4):
                if (dx, dy) != (0, 0):
                    gather[half, (dx, dy)].wait_recv()
            at = pl.ds(((X + 4 - dx) % 4) * 4, 4)
            part = kv_h[half].at[at, :, K]
            fwd[half, dx] = send(part, part, xs.at[half, dx], xr.at[half, dx], core)

    bpart = bkv.at[:, K]
    bfwd = send(bpart, bpart, es.at[4], er.at[4], core)
    for c in own_g:
        c.wait()
    bfwd.wait_recv()
    self_chunk(0)
    forward(0)
    for dx in range(4):
        fwd[0, dx].wait_recv()
    cross_all(0, 0)
    forward(1)
    for d in (1, 3):
        for kind in (4, 5, 8):
            zc[kind, d].wait_recv()

    def pair(i, _):
        cross(0, 1 + 2 * (i // READS), i % READS)
        return 0

    lax.fori_loop(0, 2 * READS, pair, 0)
    for kind in (4, 5, 8):
        zc[kind, 2].wait_recv()
    cross_all(0, 2)

    def where_read(p):
        at, has = 0, 0.0
        for j in range(READS):
            hit = reads[b, j] == p
            at = jnp.where(hit, j, at)
            has = jnp.where(hit, 1.0, has)
        return at, has

    def to_core(half):
        acc = acc_h[half]

        def one(p, _):
            at, has = where_read(p)
            cs_h[half][p] = (acc[at, :, other] * has).astype(bf16)
            return 0

        lax.fori_loop(0, PASSAGES, one, 0)
        return send(cs_h[half], cr_h[half], es.at[half], er.at[half], core)

    scattered = {}

    def to_plane(half, moved):
        moved.wait_recv()
        acc = acc_h[half]

        def one(p, _):
            at, has = where_read(p)
            ps_h[half][p] = (acc[at, :, K] * has + cr_h[half][p].astype(f32)).astype(bf16)
            return 0

        lax.fori_loop(0, PASSAGES, one, 0)
        for i, (dx, dy) in enumerate(plane):
            to = pdev(dx, dy)
            scattered[half, i] = send(
                ps_h[half].at[to[0]], pr_h[half].at[i], rs.at[half, i], rr.at[half, i], to
            )

    moved_a = to_core(0)

    for c in own_p:
        c.wait()
    for d in (1, 3, 2):
        for kind in (6, 7, 9):
            zc[kind, d].wait_recv()
    for dx in range(4):
        fwd[1, dx].wait_recv()

    def passage_chunk(step, _):
        s0, s1 = 2 * step, 2 * step + 1
        lane = lax.broadcasted_iota(jnp.int32, (512, 128), 1)
        zrow = jnp.where(lane < PROWS, (Z - s0 + 4) % 4, (Z - s1 + 4) % 4)
        row_pos = (2 * zrow + K) * PROWS + lane % PROWS
        key_pos = lax.broadcasted_iota(jnp.int32, (512, 128), 0)
        seen = (key_pos <= row_pos) & (row_pos < lens[b])
        bias = jnp.where(seen, 0.0, HIDDEN)
        pairs = jnp.concatenate([kv_a[b].reshape(256, 2 * HD), kv_b[b].reshape(256, 2 * HD)], 0)

        def rows(ref):
            parts = []
            for h in range(GROUP):
                parts.append(ref[s0, :, pl.ds(h * HD, HD)])
                parts.append(ref[s1, :, pl.ds(h * HD, HD)])
            return jnp.concatenate(parts, 0)

        stats = jnp.concatenate([pst[s0][:, :PROWS], pst[s1][:, :PROWS]], 1)
        dk, dv, part = tile(
            pairs[:, :HD], pairs[:, HD:], rows(pqa), rows(pda),
            heads_along(stats, 0), heads_along(stats, GROUP),
            jnp.concatenate([bias] * GROUP, 1),
        )
        acc_l[:, :, :, :HD] += dk.reshape(4, 2, PROWS, HD)
        acc_l[:, :, :, HD:] += dv.reshape(4, 2, PROWS, HD)
        for h in range(GROUP):
            block = (part[:, h * HD : (h + 1) * HD] * SCALE).T.astype(bf16)
            pdqs[s0, :, h * HD : (h + 1) * HD] = block[:PROWS]
            pdqs[s1, :, h * HD : (h + 1) * HD] = block[PROWS:]
        return 0

    lax.fori_loop(0, 2, passage_chunk, 0)
    ls_s[...] = acc_l[:, other].astype(bf16)
    moved_l = send(ls_s, ls_r, es.at[2], er.at[2], core)
    to_plane(0, moved_a)
    back = []

    def home(kind, slot, src, dst):
        return remote(src, dst, bs.at[kind, slot - 1], br.at[kind, slot - 1], zdev(4 - slot))

    for slot in (1, 3, 2):
        c = home(1, slot, pdqs.at[slot], pdq_o.at[:, cols(Z, WIDE)])
        c.start()
        back.append(c)
    local(pdqs.at[0], pdq_o.at[:, cols(Z, WIDE)])
    own_out = [mine[-1]]

    def finish_dq(slot):
        for h in range(GROUP):
            at = slice(h * HD, (h + 1) * HD)
            dqs[slot, :, at] = (dqt[slot, :, at] * SCALE).T.astype(bf16)

    def dq_home(slot):
        return home(0, slot, dqs.at[slot], dq_o.at[:, cols(Z, WIDE)])

    def rest(i, _):
        slot = jnp.where(i == 0, 2, 2 * i - 1)
        cross_all(1, slot)
        self_chunk(slot)
        finish_dq(slot)
        dq_home(slot).start()
        return 0

    lax.fori_loop(0, 3, rest, 0)
    ss_s[...] = acc_s[:, other].astype(bf16)
    moved_s = send(ss_s, ss_r, es.at[3], er.at[3], core)
    cross_all(1, 0)
    moved_b = to_core(1)
    finish_dq(0)
    local(dqs.at[0], dq_o.at[:, cols(Z, WIDE)])
    own_out.append(mine[-1])
    scaled = jnp.where(lax.broadcasted_iota(jnp.int32, (1, 2 * HD), 1) < HD, SCALE, 1.0)
    moved_s.wait_recv()
    fin_s[...] = ((acc_s[:, K] + ss_r[...].astype(f32)) * scaled).astype(bf16)
    to_plane(1, moved_b)

    def spread(kind, src, dk, dv):
        for d in (1, 3, 2):
            c = (Z + d) % 4
            for n, o in ((0, dk), (1, dv)):
                back.append(
                    remote(
                        src.at[c, :, n * HD : (n + 1) * HD], o.at[:, cols(Z, HD)],
                        bs.at[kind + n, d - 1], br.at[kind + n, d - 1], zdev(d),
                    )
                )
                back[-1].start()
        for n, o in ((0, dk), (1, dv)):
            own_out.append(local(src.at[Z, :, n * HD : (n + 1) * HD], o.at[:, cols(Z, HD)]))

    spread(2, fin_s, dk_o, dv_o)
    moved_l.wait_recv()
    for half in halves:
        for i in range(len(plane)):
            scattered[half, i].wait_recv()
        at, has = where_read(b)
        total = acc_h[half][at, :, K] * has + cr_h[half][b].astype(f32)
        zz = slice(2 * half, 2 * half + 2)
        total = total + acc_l[zz, K] + ls_r[zz].astype(f32)
        for i in range(len(plane)):
            total = total + pr_h[half][i].astype(f32)
        shape = (2, PROWS, 2 * HD)
        pos = (
            (2 * (lax.broadcasted_iota(jnp.int32, shape, 0) + 2 * half) + K) * PROWS
            + lax.broadcasted_iota(jnp.int32, shape, 1)
        )
        fin[zz] = jnp.where(pos < lens[b], total * scaled, 0.0).astype(bf16)
    spread(4, fin, pdk_o, pdv_o)
    for c in own_out:
        c.wait()
    for c in back:
        c.wait()
    for slot in (1, 2, 3):
        dq_home(slot).wait()
    for c in pending:
        c.wait_send()


def shards(
    query_q, query_k, query_v, query_out, query_dout, query_lse, query_seg,
    passage_q, passage_k, passage_v, passage_out, passage_dout, passage_lse,
    passage_len, reads,
):
    hbm = pl.BlockSpec(memory_space=pl.ANY)
    vmem = pl.BlockSpec(memory_space=pltpu.VMEM)
    smem = pl.BlockSpec(memory_space=pltpu.SMEM)
    pair = 2 * HD
    V = pltpu.VMEM
    dma = pltpu.SemaphoreType.DMA
    wide = H * HD
    half_shape = (PASSAGES, 2, PROWS, pair)
    scratch = [
        V((QROWS, wide), bf16), V((QROWS, wide), bf16), V((PROWS, wide), bf16), V((PROWS, wide), bf16),
        V((KVH, 16, 128), f32), V((KVH, 16, 128), f32), V((4, 16, 128), f32), V((4, 16, 128), f32),
        V((4, QROWS, WIDE), bf16), V((4, QROWS, WIDE), bf16),
        V((4, PROWS, WIDE), bf16), V((4, PROWS, WIDE), bf16),
        V((4, PROWS, pair), bf16),
        V((PASSAGES, 2, 2, PROWS, pair), bf16), V((PASSAGES, 2, 2, PROWS, pair), bf16),
        V((4, 2, QROWS, pair), bf16), V((1024, 128), f32),
        V((4, HD, WIDE), f32),
        V((READS, 2, 2, PROWS, pair), f32), V((READS, 2, 2, PROWS, pair), f32),
        V((4, 2, QROWS, pair), f32), V((4, 2, PROWS, pair), f32),
        V((4, QROWS, WIDE), bf16), V((4, PROWS, WIDE), bf16),
        V(half_shape, bf16), V(half_shape, bf16), V(half_shape, bf16), V(half_shape, bf16),
        V(half_shape, bf16), V(half_shape, bf16),
        V((15, 2, PROWS, pair), bf16), V((15, 2, PROWS, pair), bf16),
        V((4, PROWS, pair), bf16), V((4, PROWS, pair), bf16),
        V((4, QROWS, pair), bf16), V((4, QROWS, pair), bf16),
        V((4, PROWS, pair), bf16), V((4, QROWS, pair), bf16),
        dma((10, 3)), dma((10, 3)), dma((2, 15)), dma((2, 15)), dma((2, 4)), dma((2, 4)),
        dma((5,)), dma((5,)), dma((2, 15)), dma((2, 15)), dma((6, 3)), dma((6, 3)), dma((24,)),
    ]
    shape = jax.ShapeDtypeStruct
    return pl.pallas_call(
        body,
        out_shape=(
            shape((QROWS, wide), bf16), shape((QROWS, KVH * HD), bf16), shape((QROWS, KVH * HD), bf16),
            shape((PROWS, wide), bf16), shape((PROWS, KVH * HD), bf16), shape((PROWS, KVH * HD), bf16),
        ),
        in_specs=[smem, smem, hbm, hbm, hbm, hbm, hbm, vmem, vmem, hbm, hbm, hbm, hbm, hbm, vmem],
        out_specs=(hbm,) * 6,
        scratch_shapes=scratch,
        compiler_params=pltpu.CompilerParams(
            collective_id=0, has_side_effects=True, vmem_limit_bytes=60 * 2**20
        ),
    )(
        reads, passage_len,
        query_q, query_k, query_v, query_out, query_dout, query_lse, query_seg,
        passage_q, passage_k, passage_v, passage_out, passage_dout, passage_lse,
    )


def solution(mesh):
    rows = P(("pass", "query"), None)
    along = P(None, ("pass", "query"))
    return jax.shard_map(
        shards,
        mesh=mesh,
        in_specs=(
            rows, rows, rows, rows, rows, along, P("pass", None),
            rows, rows, rows, rows, rows, along, P(), P(),
        ),
        out_specs=(rows,) * 6,
        check_vma=False,
    )
```

```python
import functools
import math

import jax
import jax.numpy as jnp
from jax import lax
from jax.experimental import pallas as pl
from jax.experimental.pallas import tpu as pltpu
from jax.sharding import PartitionSpec as P

H = 32
KVH = 4
HD = 128
GROUP = H // KVH
WIDE = GROUP * HD
QROWS = 128
PROWS = 64
READS = 8
PASSAGES = 16
UNIT = 32
PARTS = ((0, 2), (2, 3), (5, 2), (7, 1))
RUNS = (
    ((0, 0, 64),),
    ((1, 0, 64), (2, 0, 32)),
    ((2, 32, 32), (3, 0, 32)),
    ((3, 32, 32),),
)
SCALE = HD ** (-0.5)
LOG2E = math.log2(math.e)
FOLD = SCALE * LOG2E
HIDDEN = -1e30
NT = (((1,), (1,)), ((), ()))
MESH = pl.DeviceIdType.MESH
f32 = jnp.float32
bf16 = jnp.bfloat16


def tile(keys, values, queries, grads, norm, delta, bias=None):
    scores = lax.dot_general(keys, queries, NT, preferred_element_type=f32)
    slopes = lax.dot_general(values, grads, NT, preferred_element_type=f32)
    power = scores * FOLD - norm
    if bias is not None:
        power = power + bias
    weight = jnp.exp2(power)
    score = (weight * (slopes - delta)).astype(bf16)
    weight = weight.astype(bf16)
    dv = jnp.dot(weight, grads, preferred_element_type=f32)
    dk = jnp.dot(score, queries, preferred_element_type=f32)
    dqt = jnp.dot(keys.T, score, preferred_element_type=f32)
    return dk, dv, dqt


def heads_down(ref, *lead):
    return jnp.concatenate([ref[(*lead, slice(None), pl.ds(h * HD, HD))] for h in range(GROUP)], 0)


def heads_along(stat, first):
    return jnp.concatenate([stat[first + h : first + h + 1, :] for h in range(GROUP)], 1)


def body(
    reads, lens,
    q, k, v, out, dout, lse, seg,
    pq, pk, pv, pout, pdout, plse,
    dq_o, dk_o, dv_o, pdq_o, pdk_o, pdv_o,
    out_v, dout_v, pout_v, pdout_v,
    stat, pstat, st, pst,
    qa, da, pqa, pda,
    pkv, shard, kv, bkv, segc,
    dqt, acc, acc_s, acc_l,
    dqs, pdqs,
    to_c, from_c, to_p, from_p,
    ls_s, ls_r, ss_s, ss_r, fin, fin_s,
    zs, zr, gs, gr, xs, xr, es, er, rs, rr, bs, br, us, ur, lo,
):
    b = lax.axis_index("pass")
    r = lax.axis_index("query")
    X, Y, Z, K = b // 4, b % 4, r // 2, r % 2
    other = 1 - K
    core = (b, Z * 2 + other)
    plane = [(dx, dy) for dx in range(4) for dy in range(4) if (dx, dy) != (0, 0)]
    pending = []
    mine = []

    def zdev(d):
        return (b, ((Z + d) % 4) * 2 + K)

    def pdev(dx, dy):
        return (((X + dx) % 4) * 4 + (Y + dy) % 4, r)

    def remote(src, dst, s, rcv, to):
        return pltpu.make_async_remote_copy(
            src_ref=src, dst_ref=dst, send_sem=s, recv_sem=rcv, device_id=to, device_id_type=MESH
        )

    def send(*args):
        c = remote(*args)
        c.start()
        pending.append(c)
        return c

    def local(src, dst):
        c = pltpu.make_async_copy(src, dst, lo.at[len(mine)])
        c.start()
        mine.append(c)
        return c

    def cols(index, width):
        return pl.ds(pl.multiple_of(index * width, width), width)

    barrier = pltpu.get_barrier_semaphore()
    greet = [zdev(d) for d in (1, 2, 3)] + [pdev(*o) for o in plane] + [core]
    for to in greet:
        pl.semaphore_signal(barrier, inc=1, device_id=to, device_id_type=MESH)
    held = [
        local(o.at[i * UNIT : (i + 1) * UNIT], pkv.at[i, :, n * KVH * HD : (n + 1) * KVH * HD])
        for n, o in ((0, pk), (1, pv))
        for i in (0, 1)
    ]
    own_d = [local(out, out_v), local(dout, dout_v), local(pout, pout_v), local(pdout, pdout_v)]
    own_q = [
        local(k.at[:, cols(Z, HD)], bkv.at[Z, K, :, 0:HD]),
        local(v.at[:, cols(Z, HD)], bkv.at[Z, K, :, HD : 2 * HD]),
        local(q.at[:, cols(Z, WIDE)], qa.at[0]),
        local(dout.at[:, cols(Z, WIDE)], da.at[0]),
    ]
    own_p = [
        local(pq.at[:, cols(Z, WIDE)], pqa.at[0]),
        local(pdout.at[:, cols(Z, WIDE)], pda.at[0]),
    ]

    for block in range(8):
        row = seg[:, block * 128 : (block + 1) * 128].astype(f32)
        segc[block * 128 : (block + 1) * 128, :] = jnp.broadcast_to(row, (128, 128)).T
    for c in held:
        c.wait()
    shard[pl.ds(2 * Z, 2), :, 0:HD] = pkv[:, :, cols(Z, HD)]
    shard[pl.ds(2 * Z, 2), :, HD : 2 * HD] = pkv[:, :, cols(KVH + Z, HD)]
    pl.semaphore_wait(barrier, len(greet))

    def z_copy(kind, d):
        c = (Z + d) % 4
        src, dst = (
            (pkv.at[:, :, cols(c, HD)], shard.at[pl.ds(2 * Z, 2), :, 0:HD]),
            (pkv.at[:, :, cols(KVH + c, HD)], shard.at[pl.ds(2 * Z, 2), :, HD : 2 * HD]),
            (k.at[:, cols(c, HD)], bkv.at[Z, K, :, 0:HD]),
            (v.at[:, cols(c, HD)], bkv.at[Z, K, :, HD : 2 * HD]),
            (q.at[:, cols(c, WIDE)], qa.at[d]),
            (dout.at[:, cols(c, WIDE)], da.at[d]),
            (pq.at[:, cols(c, WIDE)], pqa.at[d]),
            (pdout.at[:, cols(c, WIDE)], pda.at[d]),
            (stat.at[c], st.at[d]),
            (pstat.at[c], pst.at[d]),
        )[kind]
        return remote(src, dst, zs.at[kind, d - 1], zr.at[kind, d - 1], zdev(d))

    def z_out(kinds, offsets):
        for d in offsets:
            for kind in kinds:
                c = z_copy(kind, d)
                c.start()
                pending.append(c)

    def z_in(kinds, offsets):
        for d in offsets:
            for kind in kinds:
                z_copy(kind, d).wait_recv()

    z_out((0, 1), (1, 3, 2))
    z_out((2, 3), (1, 3, 2))

    z_in((0, 1), (1, 3, 2))
    gather, own_g = {}, {}

    def plane_out(n):
        first, count = PARTS[n]
        src = shard.at[first : first + count]
        dst = kv[n].at[b, :, K]
        own_g[n] = local(src, dst)
        for i, o in enumerate(plane):
            gather[n, o] = send(src, dst, gs.at[n, i], gr.at[n, i], pdev(*o))

    fwd = {}

    def forward(n):
        own_g[n].wait()
        for dx in range(4):
            for dy in range(4):
                if (dx, dy) != (0, 0):
                    gather[n, (dx, dy)].wait_recv()
            at = pl.ds(((X + 4 - dx) % 4) * 4, 4)
            part = kv[n].at[at, :, K]
            fwd[n, dx] = send(part, part, xs.at[n, dx], xr.at[n, dx], core)

    def forwarded(n):
        for dx in range(4):
            fwd[n, dx].wait_recv()

    plane_out(0)
    z_out((4, 5), (1, 3))
    pstat[...] = jnp.zeros_like(pstat)
    for c in own_d:
        c.wait()

    def group_stats(c, _):
        at8 = pl.ds(pl.multiple_of(c * GROUP, GROUP), GROUP)
        stat[c, 0:GROUP, :] = lse[at8, :] * LOG2E
        pstat[c, 0:GROUP, 0:PROWS] = plse[at8, :] * LOG2E
        for h in range(GROUP):
            at = pl.ds(pl.multiple_of(c * WIDE + h * HD, HD), HD)
            prod = dout_v[:, at].astype(f32) * out_v[:, at].astype(f32)
            stat[c, GROUP + h : GROUP + h + 1, :] = jnp.sum(prod.T, axis=0, keepdims=True)
            prod = pdout_v[:, at].astype(f32) * pout_v[:, at].astype(f32)
            pstat[c, GROUP + h : GROUP + h + 1, 0:PROWS] = jnp.sum(prod.T, axis=0, keepdims=True)
        return 0

    lax.fori_loop(0, KVH, group_stats, 0)
    st[0] = stat[Z]
    pst[0] = pstat[Z]
    z_out((8, 9), (1, 3, 2))
    for ref in (dqt, *acc, acc_s, acc_l):
        ref[...] = jnp.zeros_like(ref)

    for c in own_q:
        c.wait()
    z_in((2, 3), (1, 3, 2))
    part = bkv.at[:, K]
    bfwd = send(part, part, es.at[5], er.at[5], core)
    plane_out(1)

    def self_chunk(slot):
        rb = ((Z - slot + 4) % 4) * 2 + K
        first = jnp.clip(rb - 4, 0, 3)
        start = pl.multiple_of(first * 128, 128)
        at = pl.ds(start, 640)
        key_pos = start + lax.broadcasted_iota(jnp.int32, (640, 128), 0)
        row_pos = rb * 128 + lax.broadcasted_iota(jnp.int32, (640, 128), 1)
        row_seg = seg[:, pl.ds(pl.multiple_of(rb * 128, 128), 128)].astype(f32)
        seen = (key_pos <= row_pos) & (segc[at, :] == row_seg)
        bias = jnp.where(seen, 0.0, HIDDEN)
        pairs = jnp.concatenate([bkv[(first + i) // 2, (first + i) % 2] for i in range(5)], 0)
        dk, dv, part = tile(
            pairs[:, :HD], pairs[:, HD:], heads_down(qa, slot), heads_down(da, slot),
            heads_along(st[slot], 0), heads_along(st[slot], GROUP),
            jnp.concatenate([bias] * GROUP, 1),
        )
        dqt[slot] += part
        for i in range(5):
            zi, ki = (first + i) // 2, (first + i) % 2
            acc_s[zi, ki, :, :HD] += dk[i * 128 : (i + 1) * 128]
            acc_s[zi, ki, :, HD:] += dv[i * 128 : (i + 1) * 128]

    def places(first, shape):
        row = lax.broadcasted_iota(jnp.int32, shape, 0)
        unit = first + row // (2 * UNIT)
        return unit // 2 * 128 + row // UNIT % 2 * 64 + unit % 2 * UNIT + row % UNIT

    def cross(n, slot):
        first, count = PARTS[n]
        rows = count * 2 * UNIT
        abreast = -(-256 // rows)

        def one(t, _):
            pairs = []
            for i in range(abreast):
                p = reads[t * abreast + i, b]
                pair = kv[n][p].reshape(rows, 2 * HD)
                if first + count > 6:
                    seen = places(first, (rows, 2 * HD)) < lens[p]
                    pair = jnp.where(seen, pair.astype(f32), 0.0).astype(bf16)
                pairs.append(pair)
            pairs = jnp.concatenate(pairs, 0)
            dk, dv, part = tile(
                pairs[:, :HD], pairs[:, HD:], heads_down(qa, slot), heads_down(da, slot),
                heads_along(st[slot], 0), heads_along(st[slot], GROUP),
            )
            dqt[slot] += part
            at = pl.ds(t * abreast, abreast)
            acc[n][at, :, :, :, :HD] += dk.reshape(abreast, count, 2, UNIT, HD)
            acc[n][at, :, :, :, HD:] += dv.reshape(abreast, count, 2, UNIT, HD)
            return 0

        lax.fori_loop(0, READS // abreast, one, 0)

    def where_read(p):
        at, has = 0, 0.0
        for j in range(READS):
            hit = reads[j, b] == p
            at = jnp.where(hit, j, at)
            has = jnp.where(hit, 1.0, has)
        return at, has

    moved = {}

    def to_core(n):
        def one(p, _):
            at, has = where_read(p)
            to_c[n][p] = (acc[n][at, :, other] * has).astype(bf16)
            return 0

        lax.fori_loop(0, PASSAGES, one, 0)
        moved[n] = send(to_c[n], from_c[n], es.at[n], er.at[n], core)

    scattered = {}

    def to_plane(n):
        moved[n].wait_recv()

        def one(p, _):
            at, has = where_read(p)
            to_p[n][p] = (acc[n][at, :, K] * has + from_c[n][p].astype(f32)).astype(bf16)
            return 0

        lax.fori_loop(0, PASSAGES, one, 0)
        for i, (dx, dy) in enumerate(plane):
            to = pdev(dx, dy)
            scattered[n, i] = send(
                to_p[n].at[to[0]], from_p[n].at[i], rs.at[n, i], rr.at[n, i], to
            )

    def passage_chunk(step, _):
        s0, s1 = 2 * step, 2 * step + 1
        lane = lax.broadcasted_iota(jnp.int32, (512, 128), 1)
        zrow = jnp.where(lane < PROWS, (Z - s0 + 4) % 4, (Z - s1 + 4) % 4)
        row_pos = (2 * zrow + K) * PROWS + lane % PROWS
        key_pos = places(0, (512, 128))
        seen = (key_pos <= row_pos) & (row_pos < lens[b])
        bias = jnp.where(seen, 0.0, HIDDEN)
        pairs = jnp.concatenate([ref[b].reshape(-1, 2 * HD) for ref in kv], 0)

        def rows(ref):
            parts = []
            for h in range(GROUP):
                parts.append(ref[s0, :, pl.ds(h * HD, HD)])
                parts.append(ref[s1, :, pl.ds(h * HD, HD)])
            return jnp.concatenate(parts, 0)

        stats = jnp.concatenate([pst[s0][:, :PROWS], pst[s1][:, :PROWS]], 1)
        dk, dv, part = tile(
            pairs[:, :HD], pairs[:, HD:], rows(pqa), rows(pda),
            heads_along(stats, 0), heads_along(stats, GROUP),
            jnp.concatenate([bias] * GROUP, 1),
        )
        acc_l[:, :, :, :HD] += dk.reshape(8, 2, UNIT, HD)
        acc_l[:, :, :, HD:] += dv.reshape(8, 2, UNIT, HD)
        for h in range(GROUP):
            block = (part[:, h * HD : (h + 1) * HD] * SCALE).T.astype(bf16)
            pdqs[s0, :, h * HD : (h + 1) * HD] = block[:PROWS]
            pdqs[s1, :, h * HD : (h + 1) * HD] = block[PROWS:]
        return 0

    def home(kind, slot, src, dst):
        return remote(src, dst, bs.at[kind, slot - 1], br.at[kind, slot - 1], zdev(4 - slot))

    def finish_dq(slot):
        for h in range(GROUP):
            at = slice(h * HD, (h + 1) * HD)
            dqs[slot, :, at] = (dqt[slot, :, at] * SCALE).T.astype(bf16)

    def dq_home(slot):
        return home(0, slot, dqs.at[slot], dq_o.at[:, cols(Z, WIDE)])

    back, own_out = [], []

    def spread(kind, src, dk, dv):
        for d in (1, 3, 2):
            c = (Z + d) % 4
            for n, o in ((0, dk), (1, dv)):
                back.append(
                    remote(
                        src.at[c, :, n * HD : (n + 1) * HD], o.at[:, cols(Z, HD)],
                        bs.at[kind + n, d - 1], br.at[kind + n, d - 1], zdev(d),
                    )
                )
                back[-1].start()
        for n, o in ((0, dk), (1, dv)):
            own_out.append(local(src.at[Z, :, n * HD : (n + 1) * HD], o.at[:, cols(Z, HD)]))

    scaled = jnp.where(lax.broadcasted_iota(jnp.int32, (1, 2 * HD), 1) < HD, SCALE, 1.0)
    runs = [(n, run) for n in range(len(PARTS)) for run in RUNS[n]]

    def run_copy(i, which):
        chip, row, rows = runs[i][1]
        src = fin.at[chip, row : row + rows, which * HD : (which + 1) * HD]
        dst = (pdk_o, pdv_o)[which].at[row : row + rows, cols(Z, HD)]
        return src, dst, chip

    def run_remote(i, which, d):
        src, dst, chip = run_copy(i, which)
        at = 2 * i + which
        return remote(src, dst, us.at[at, d - 1], ur.at[at, d - 1], (b, chip * 2 + K))

    def run_local(i, which):
        src, dst, chip = run_copy(i, which)
        return pltpu.make_async_copy(src, dst, us.at[2 * i + which, 3])

    def final(n):
        first, count = PARTS[n]
        for i in range(len(plane)):
            scattered[n, i].wait_recv()
        at, has = where_read(b)
        units = slice(first, first + count)
        total = acc[n][at, :, K] * has + from_c[n][b].astype(f32)
        total = total + acc_l[units, K] + ls_r[units].astype(f32)
        for i in range(len(plane)):
            total = total + from_p[n][i].astype(f32)
        total = total * scaled
        for u in range(count):
            chip, row = (first + u) // 2, (first + u) % 2 * UNIT
            pos = chip * 128 + K * 64 + row
            pos = pos + lax.broadcasted_iota(jnp.int32, (UNIT, 2 * HD), 0)
            fin[chip, row : row + UNIT, :] = jnp.where(pos < lens[b], total[u], 0.0).astype(bf16)
        for i, (part, (chip, _, _)) in enumerate(runs):
            if part == n:
                @pl.when(Z != chip)
                def _():
                    for which in (0, 1):
                        run_remote(i, which, (chip - Z + 4) % 4).start()

                @pl.when(Z == chip)
                def _():
                    for which in (0, 1):
                        run_local(i, which).start()

    def finals_done():
        for i, (_, (chip, _, _)) in enumerate(runs):
            @pl.when(Z != chip)
            def _():
                for which in (0, 1):
                    run_remote(i, which, (chip - Z + 4) % 4).wait_send()

            @pl.when(Z == chip)
            def _():
                for which in (0, 1):
                    run_local(i, which).wait()
                    for d in (1, 2, 3):
                        run_remote(i, which, d).wait_recv()

    def chunks(n, slots):
        count, slot_of = slots

        def one(i, _):
            cross(n, slot_of(i))
            return 0

        lax.fori_loop(0, count, one, 0)

    forward(0)
    z_out((4, 5), (2,))
    bfwd.wait_recv()
    self_chunk(0)
    forwarded(0)
    cross(0, 0)
    z_in((4, 5, 8), (1, 3))
    chunks(0, (2, lambda i: 1 + 2 * i))

    def self_near(i, _):
        self_chunk(1 + 2 * i)
        return 0

    lax.fori_loop(0, 2, self_near, 0)
    forward(1)
    plane_out(2)
    forwarded(1)
    cross(1, 0)
    z_in((4, 5, 8), (2,))
    z_out((6, 7), (1, 3, 2))
    cross(0, 2)
    to_core(0)
    cross(1, 1)
    to_plane(0)
    chunks(1, (2, lambda i: 3 - i))
    to_core(1)
    self_chunk(2)
    forward(2)
    plane_out(3)
    forwarded(2)
    cross(2, 0)
    to_plane(1)
    chunks(2, (3, lambda i: i + 1))
    to_core(2)
    forward(3)
    for c in own_p:
        c.wait()
    z_in((6, 7, 9), (1, 3, 2))
    forwarded(3)
    lax.fori_loop(0, 2, passage_chunk, 0)
    to_plane(2)
    for slot in (1, 3, 2):
        c = home(1, slot, pdqs.at[slot], pdq_o.at[:, cols(Z, WIDE)])
        c.start()
        back.append(c)
    own_out.append(local(pdqs.at[0], pdq_o.at[:, cols(Z, WIDE)]))
    ls_s[...] = acc_l[:, other].astype(bf16)
    moved_l = send(ls_s, ls_r, es.at[6], er.at[6], core)
    ss_s[...] = acc_s[:, other].astype(bf16)
    moved_s = send(ss_s, ss_r, es.at[4], er.at[4], core)

    def last_part(i, _):
        slot = jnp.where(i == 0, 2, 2 * i - 1)
        cross(3, slot)
        finish_dq(slot)
        dq_home(slot).start()
        return 0

    lax.fori_loop(0, 3, last_part, 0)
    cross(3, 0)
    to_core(3)
    finish_dq(0)
    own_out.append(local(dqs.at[0], dq_o.at[:, cols(Z, WIDE)]))
    moved_l.wait_recv()
    final(0)
    to_plane(3)
    moved_s.wait_recv()
    fin_s[...] = ((acc_s[:, K] + ss_r[...].astype(f32)) * scaled).astype(bf16)
    spread(2, fin_s, dk_o, dv_o)
    final(1)
    final(2)
    final(3)
    finals_done()
    for c in own_out:
        c.wait()
    for c in back:
        c.wait()
    for slot in (1, 2, 3):
        dq_home(slot).wait()
    for c in pending:
        c.wait_send()


def place(*refs):
    count = (len(refs) - 1) // 3
    ins, outs, held, sems = refs[:count], refs[count : 2 * count], refs[2 * count : -1], refs[-1]
    there = [pltpu.make_async_copy(ins[i], held[i], sems.at[0, i]) for i in range(count)]
    away = [pltpu.make_async_copy(held[i], outs[i], sems.at[1, i]) for i in range(count)]
    for c in there:
        c.start()
    for i in range(count):
        there[i].wait()
        away[i].start()
    for c in away:
        c.wait()


def shards(
    query_q, query_k, query_v, query_out, query_dout, query_lse, query_seg,
    passage_q, passage_k, passage_v, passage_out, passage_dout, passage_lse,
    passage_len, reads,
):
    hbm = pl.BlockSpec(memory_space=pl.ANY)
    vmem = pl.BlockSpec(memory_space=pltpu.VMEM)
    smem = pl.BlockSpec(memory_space=pltpu.SMEM)
    pair = 2 * HD
    V = pltpu.VMEM
    dma = pltpu.SemaphoreType.DMA
    wide = H * HD
    counts = [count for _, count in PARTS]
    parts = len(counts)
    stats = V((4, 16, 128), f32)
    scratch = [
        V((QROWS, wide), bf16), V((QROWS, wide), bf16), V((PROWS, wide), bf16), V((PROWS, wide), bf16),
        stats, stats, stats, stats,
        V((4, QROWS, WIDE), bf16), V((4, QROWS, WIDE), bf16),
        V((4, PROWS, WIDE), bf16), V((4, PROWS, WIDE), bf16),
        V((2, UNIT, 2 * KVH * HD), bf16), V((8, UNIT, pair), bf16),
        [V((PASSAGES, n, 2, UNIT, pair), bf16) for n in counts],
        V((4, 2, QROWS, pair), bf16), V((1024, 128), f32),
        V((4, HD, WIDE), f32),
        [V((READS, n, 2, UNIT, pair), f32) for n in counts],
        V((4, 2, QROWS, pair), f32), V((8, 2, UNIT, pair), f32),
        V((4, QROWS, WIDE), bf16), V((4, PROWS, WIDE), bf16),
        [V((PASSAGES, n, UNIT, pair), bf16) for n in counts],
        [V((PASSAGES, n, UNIT, pair), bf16) for n in counts],
        [V((PASSAGES, n, UNIT, pair), bf16) for n in counts],
        [V((PASSAGES - 1, n, UNIT, pair), bf16) for n in counts],
        V((8, UNIT, pair), bf16), V((8, UNIT, pair), bf16),
        V((4, QROWS, pair), bf16), V((4, QROWS, pair), bf16),
        V((4, PROWS, pair), bf16), V((4, QROWS, pair), bf16),
        dma((10, 3)), dma((10, 3)), dma((parts, 15)), dma((parts, 15)),
        dma((parts, 4)), dma((parts, 4)),
        dma((7,)), dma((7,)), dma((parts, 15)), dma((parts, 15)), dma((4, 3)), dma((4, 3)),
        dma((12, 4)), dma((12, 3)), dma((24,)),
    ]
    shape = jax.ShapeDtypeStruct
    results = (
        shape((QROWS, wide), bf16), shape((QROWS, KVH * HD), bf16), shape((QROWS, KVH * HD), bf16),
        shape((PROWS, wide), bf16), shape((PROWS, KVH * HD), bf16), shape((PROWS, KVH * HD), bf16),
    )
    found = pl.pallas_call(
        body,
        out_shape=results,
        in_specs=[smem, smem, hbm, hbm, hbm, hbm, hbm, vmem, vmem, hbm, hbm, hbm, hbm, hbm, vmem],
        out_specs=(hbm,) * 6,
        scratch_shapes=scratch,
        compiler_params=pltpu.CompilerParams(
            collective_id=0, has_side_effects=True, vmem_limit_bytes=60 * 2**20
        ),
    )(
        reads.T, passage_len,
        query_q, query_k, query_v, query_out, query_dout, query_lse, query_seg,
        passage_q, passage_k, passage_v, passage_out, passage_dout, passage_lse,
    )
    return pl.pallas_call(
        place,
        out_shape=results,
        in_specs=[hbm] * 6,
        out_specs=(hbm,) * 6,
        scratch_shapes=[V(x.shape, bf16) for x in results] + [dma((2, 6))],
    )(*found)


def solution(mesh):
    rows = P(("pass", "query"), None)
    along = P(None, ("pass", "query"))
    return jax.shard_map(
        shards,
        mesh=mesh,
        in_specs=(
            rows, rows, rows, rows, rows, along, P("pass", None),
            rows, rows, rows, rows, rows, along, P(), P(),
        ),
        out_specs=(rows,) * 6,
        check_vma=False,
    )
```

```python
import functools
import math

import jax
import jax.numpy as jnp
from jax import lax
from jax.experimental import pallas as pl
from jax.experimental.pallas import tpu as pltpu
from jax.sharding import PartitionSpec as P

H = 32
KVH = 4
HD = 128
GROUP = H // KVH
WIDE = GROUP * HD
QROWS = 128
PROWS = 64
READS = 8
PASSAGES = 16
UNIT = 32
PARTS = ((0, 2), (2, 3), (5, 2), (7, 1))
RUNS = (
    ((0, 0, 64),),
    ((1, 0, 64), (2, 0, 32)),
    ((2, 32, 32), (3, 0, 32)),
    ((3, 32, 32),),
)
SCALE = HD ** (-0.5)
LOG2E = math.log2(math.e)
FOLD = SCALE * LOG2E
HIDDEN = -1e30
NT = (((1,), (1,)), ((), ()))
MESH = pl.DeviceIdType.MESH
f32 = jnp.float32
bf16 = jnp.bfloat16


def tile(keys, values, queries, grads, norm, delta, bias=None):
    scores = lax.dot_general(keys, queries, NT, preferred_element_type=f32)
    slopes = lax.dot_general(values, grads, NT, preferred_element_type=f32)
    power = scores * FOLD - norm
    if bias is not None:
        power = power + bias
    weight = jnp.exp2(power)
    score = (weight * (slopes - delta)).astype(bf16)
    weight = weight.astype(bf16)
    dv = jnp.dot(weight, grads, preferred_element_type=f32)
    dk = jnp.dot(score, queries, preferred_element_type=f32)
    dqt = jnp.dot(keys.T, score, preferred_element_type=f32)
    return dk, dv, dqt


def heads_down(ref, *lead):
    return jnp.concatenate([ref[(*lead, slice(None), pl.ds(h * HD, HD))] for h in range(GROUP)], 0)


def heads_along(stat, first):
    return jnp.concatenate([stat[first + h : first + h + 1, :] for h in range(GROUP)], 1)


def body(
    reads, lens,
    q, k, v, out, dout, lse, seg,
    pq, pk, pv, pout, pdout, plse,
    dq_o, dk_o, dv_o, pdq_o, pdk_o, pdv_o,
    out_v, dout_v, pout_v, pdout_v,
    stat, pstat, st, pst,
    qa, da, pqa, pda,
    pkv, shard, kv, bkv, segc,
    dqt, acc, acc_s, acc_l,
    dqs, pdqs,
    to_c, from_c, to_p, from_p,
    ls_s, ls_r, ss_s, ss_r, fin, fin_s,
    zs, zr, gs, gr, xs, xr, es, er, rs, rr, bs, br, us, ur, lo,
):
    b = lax.axis_index("pass")
    r = lax.axis_index("query")
    X, Y, Z, K = b // 4, b % 4, r // 2, r % 2
    other = 1 - K
    core = (b, Z * 2 + other)
    plane = [(dx, dy) for dx in range(4) for dy in range(4) if (dx, dy) != (0, 0)]
    pending = []
    mine = []

    def zdev(d):
        return (b, ((Z + d) % 4) * 2 + K)

    def pdev(dx, dy):
        return (((X + dx) % 4) * 4 + (Y + dy) % 4, r)

    def remote(src, dst, s, rcv, to):
        return pltpu.make_async_remote_copy(
            src_ref=src, dst_ref=dst, send_sem=s, recv_sem=rcv, device_id=to, device_id_type=MESH
        )

    def send(*args):
        c = remote(*args)
        c.start()
        pending.append(c)
        return c

    def local(src, dst):
        c = pltpu.make_async_copy(src, dst, lo.at[len(mine)])
        c.start()
        mine.append(c)
        return c

    def cols(index, width):
        return pl.ds(pl.multiple_of(index * width, width), width)

    barrier = pltpu.get_barrier_semaphore()
    greet = [zdev(d) for d in (1, 2, 3)] + [pdev(*o) for o in plane] + [core]
    for to in greet:
        pl.semaphore_signal(barrier, inc=1, device_id=to, device_id_type=MESH)
    held = [
        local(o.at[i * UNIT : (i + 1) * UNIT], pkv.at[i, :, n * KVH * HD : (n + 1) * KVH * HD])
        for n, o in ((0, pk), (1, pv))
        for i in (0, 1)
    ]
    own_d = [local(out, out_v), local(dout, dout_v), local(pout, pout_v), local(pdout, pdout_v)]
    own_q = [
        local(k.at[:, cols(Z, HD)], bkv.at[Z, K, :, 0:HD]),
        local(v.at[:, cols(Z, HD)], bkv.at[Z, K, :, HD : 2 * HD]),
        local(q.at[:, cols(Z, WIDE)], qa.at[0]),
        local(dout.at[:, cols(Z, WIDE)], da.at[0]),
    ]
    own_p = [
        local(pq.at[:, cols(Z, WIDE)], pqa.at[0]),
        local(pdout.at[:, cols(Z, WIDE)], pda.at[0]),
    ]

    for block in range(8):
        row = seg[:, block * 128 : (block + 1) * 128].astype(f32)
        segc[block * 128 : (block + 1) * 128, :] = jnp.broadcast_to(row, (128, 128)).T
    for c in held:
        c.wait()
    shard[pl.ds(2 * Z, 2), :, 0:HD] = pkv[:, :, cols(Z, HD)]
    shard[pl.ds(2 * Z, 2), :, HD : 2 * HD] = pkv[:, :, cols(KVH + Z, HD)]
    pl.semaphore_wait(barrier, len(greet))

    def z_copy(kind, d):
        c = (Z + d) % 4
        src, dst = (
            (pkv.at[:, :, cols(c, HD)], shard.at[pl.ds(2 * Z, 2), :, 0:HD]),
            (pkv.at[:, :, cols(KVH + c, HD)], shard.at[pl.ds(2 * Z, 2), :, HD : 2 * HD]),
            (k.at[:, cols(c, HD)], bkv.at[Z, K, :, 0:HD]),
            (v.at[:, cols(c, HD)], bkv.at[Z, K, :, HD : 2 * HD]),
            (q.at[:, cols(c, WIDE)], qa.at[d]),
            (dout.at[:, cols(c, WIDE)], da.at[d]),
            (pq.at[:, cols(c, WIDE)], pqa.at[d]),
            (pdout.at[:, cols(c, WIDE)], pda.at[d]),
            (stat.at[c], st.at[d]),
            (pstat.at[c], pst.at[d]),
        )[kind]
        return remote(src, dst, zs.at[kind, d - 1], zr.at[kind, d - 1], zdev(d))

    def z_out(kinds, offsets):
        for d in offsets:
            for kind in kinds:
                c = z_copy(kind, d)
                c.start()
                pending.append(c)

    def z_in(kinds, offsets):
        for d in offsets:
            for kind in kinds:
                z_copy(kind, d).wait_recv()

    z_out((0, 1), (1, 3, 2))
    z_out((2, 3), (1, 3, 2))

    z_in((0, 1), (1, 3, 2))
    gather, own_g = {}, {}

    def plane_out(n):
        first, count = PARTS[n]
        src = shard.at[first : first + count]
        dst = kv[n].at[b, :, K]
        own_g[n] = local(src, dst)
        for i, o in enumerate(plane):
            gather[n, o] = send(src, dst, gs.at[n, i], gr.at[n, i], pdev(*o))

    fwd = {}

    def forward(n):
        own_g[n].wait()
        for dx in range(4):
            for dy in range(4):
                if (dx, dy) != (0, 0):
                    gather[n, (dx, dy)].wait_recv()
            at = pl.ds(((X + 4 - dx) % 4) * 4, 4)
            part = kv[n].at[at, :, K]
            fwd[n, dx] = send(part, part, xs.at[n, dx], xr.at[n, dx], core)

    def forwarded(n):
        for dx in range(4):
            fwd[n, dx].wait_recv()

    plane_out(0)
    z_out((4, 5), (1, 3))
    pstat[...] = jnp.zeros_like(pstat)
    for c in own_d:
        c.wait()

    def group_stats(c, _):
        at8 = pl.ds(pl.multiple_of(c * GROUP, GROUP), GROUP)
        stat[c, 0:GROUP, :] = lse[at8, :] * LOG2E
        pstat[c, 0:GROUP, 0:PROWS] = plse[at8, :] * LOG2E
        for h in range(GROUP):
            at = pl.ds(pl.multiple_of(c * WIDE + h * HD, HD), HD)
            prod = dout_v[:, at].astype(f32) * out_v[:, at].astype(f32)
            stat[c, GROUP + h : GROUP + h + 1, :] = jnp.sum(prod.T, axis=0, keepdims=True)
            prod = pdout_v[:, at].astype(f32) * pout_v[:, at].astype(f32)
            pstat[c, GROUP + h : GROUP + h + 1, 0:PROWS] = jnp.sum(prod.T, axis=0, keepdims=True)
        return 0

    lax.fori_loop(0, KVH, group_stats, 0)
    st[0] = stat[Z]
    pst[0] = pstat[Z]
    z_out((8, 9), (1, 3, 2))
    for ref in (dqt, *acc, acc_s, acc_l):
        ref[...] = jnp.zeros_like(ref)

    for c in own_q:
        c.wait()
    z_in((2, 3), (1, 3, 2))
    part = bkv.at[:, K]
    bfwd = send(part, part, es.at[5], er.at[5], core)
    plane_out(1)

    def self_chunk(slot):
        rb = ((Z - slot + 4) % 4) * 2 + K
        first = jnp.clip(rb - 4, 0, 3)
        start = pl.multiple_of(first * 128, 128)
        at = pl.ds(start, 640)
        key_pos = start + lax.broadcasted_iota(jnp.int32, (640, 128), 0)
        row_pos = rb * 128 + lax.broadcasted_iota(jnp.int32, (640, 128), 1)
        row_seg = seg[:, pl.ds(pl.multiple_of(rb * 128, 128), 128)].astype(f32)
        seen = (key_pos <= row_pos) & (segc[at, :] == row_seg)
        bias = jnp.where(seen, 0.0, HIDDEN)
        pairs = jnp.concatenate([bkv[(first + i) // 2, (first + i) % 2] for i in range(5)], 0)
        dk, dv, part = tile(
            pairs[:, :HD], pairs[:, HD:], heads_down(qa, slot), heads_down(da, slot),
            heads_along(st[slot], 0), heads_along(st[slot], GROUP),
            jnp.concatenate([bias] * GROUP, 1),
        )
        dqt[slot] += part
        for i in range(5):
            zi, ki = (first + i) // 2, (first + i) % 2
            acc_s[zi, ki, :, :HD] += dk[i * 128 : (i + 1) * 128]
            acc_s[zi, ki, :, HD:] += dv[i * 128 : (i + 1) * 128]

    def places(first, shape):
        row = lax.broadcasted_iota(jnp.int32, shape, 0)
        unit = first + row // (2 * UNIT)
        return unit // 2 * 128 + row // UNIT % 2 * 64 + unit % 2 * UNIT + row % UNIT

    def cross(n, slot):
        first, count = PARTS[n]
        rows = count * 2 * UNIT
        abreast = -(-256 // rows)

        def one(t, _):
            pairs = []
            for i in range(abreast):
                p = reads[t * abreast + i, b]
                pair = kv[n][p].reshape(rows, 2 * HD)
                if first + count > 6:
                    seen = places(first, (rows, 2 * HD)) < lens[p]
                    pair = jnp.where(seen, pair.astype(f32), 0.0).astype(bf16)
                pairs.append(pair)
            pairs = jnp.concatenate(pairs, 0)
            dk, dv, part = tile(
                pairs[:, :HD], pairs[:, HD:], heads_down(qa, slot), heads_down(da, slot),
                heads_along(st[slot], 0), heads_along(st[slot], GROUP),
            )
            dqt[slot] += part
            at = pl.ds(t * abreast, abreast)
            acc[n][at, :, :, :, :HD] += dk.reshape(abreast, count, 2, UNIT, HD)
            acc[n][at, :, :, :, HD:] += dv.reshape(abreast, count, 2, UNIT, HD)
            return 0

        lax.fori_loop(0, READS // abreast, one, 0)

    def where_read(p):
        at, has = 0, 0.0
        for j in range(READS):
            hit = reads[j, b] == p
            at = jnp.where(hit, j, at)
            has = jnp.where(hit, 1.0, has)
        return at, has

    moved = {}

    def to_core(n):
        def one(p, _):
            at, has = where_read(p)
            to_c[n][p] = (acc[n][at, :, other] * has).astype(bf16)
            return 0

        lax.fori_loop(0, PASSAGES, one, 0, unroll=4)
        moved[n] = send(to_c[n], from_c[n], es.at[n], er.at[n], core)

    scattered = {}

    def to_plane(n):
        moved[n].wait_recv()

        def one(p, _):
            at, has = where_read(p)
            to_p[n][p] = (acc[n][at, :, K] * has + from_c[n][p].astype(f32)).astype(bf16)
            return 0

        lax.fori_loop(0, PASSAGES, one, 0, unroll=4)
        for i, (dx, dy) in enumerate(plane):
            to = pdev(dx, dy)
            scattered[n, i] = send(
                to_p[n].at[to[0]], from_p[n].at[i], rs.at[n, i], rr.at[n, i], to
            )

    def passage_chunk(step, _):
        s0, s1 = 2 * step, 2 * step + 1
        lane = lax.broadcasted_iota(jnp.int32, (512, 128), 1)
        zrow = jnp.where(lane < PROWS, (Z - s0 + 4) % 4, (Z - s1 + 4) % 4)
        row_pos = (2 * zrow + K) * PROWS + lane % PROWS
        key_pos = places(0, (512, 128))
        seen = (key_pos <= row_pos) & (row_pos < lens[b])
        bias = jnp.where(seen, 0.0, HIDDEN)
        pairs = jnp.concatenate([ref[b].reshape(-1, 2 * HD) for ref in kv], 0)

        def rows(ref):
            parts = []
            for h in range(GROUP):
                parts.append(ref[s0, :, pl.ds(h * HD, HD)])
                parts.append(ref[s1, :, pl.ds(h * HD, HD)])
            return jnp.concatenate(parts, 0)

        stats = jnp.concatenate([pst[s0][:, :PROWS], pst[s1][:, :PROWS]], 1)
        dk, dv, part = tile(
            pairs[:, :HD], pairs[:, HD:], rows(pqa), rows(pda),
            heads_along(stats, 0), heads_along(stats, GROUP),
            jnp.concatenate([bias] * GROUP, 1),
        )
        acc_l[:, :, :, :HD] += dk.reshape(8, 2, UNIT, HD)
        acc_l[:, :, :, HD:] += dv.reshape(8, 2, UNIT, HD)
        for h in range(GROUP):
            block = (part[:, h * HD : (h + 1) * HD] * SCALE).T.astype(bf16)
            pdqs[s0, :, h * HD : (h + 1) * HD] = block[:PROWS]
            pdqs[s1, :, h * HD : (h + 1) * HD] = block[PROWS:]
        return 0

    def home(kind, slot, src, dst):
        return remote(src, dst, bs.at[kind, slot - 1], br.at[kind, slot - 1], zdev(4 - slot))

    def finish_dq(slot):
        for h in range(GROUP):
            at = slice(h * HD, (h + 1) * HD)
            dqs[slot, :, at] = (dqt[slot, :, at] * SCALE).T.astype(bf16)

    def dq_home(slot):
        return home(0, slot, dqs.at[slot], dq_o.at[:, cols(Z, WIDE)])

    back, own_out = [], []

    def spread(kind, src, dk, dv):
        for d in (1, 3, 2):
            c = (Z + d) % 4
            for n, o in ((0, dk), (1, dv)):
                back.append(
                    remote(
                        src.at[c, :, n * HD : (n + 1) * HD], o.at[:, cols(Z, HD)],
                        bs.at[kind + n, d - 1], br.at[kind + n, d - 1], zdev(d),
                    )
                )
                back[-1].start()
        for n, o in ((0, dk), (1, dv)):
            own_out.append(local(src.at[Z, :, n * HD : (n + 1) * HD], o.at[:, cols(Z, HD)]))

    scaled = jnp.where(lax.broadcasted_iota(jnp.int32, (1, 2 * HD), 1) < HD, SCALE, 1.0)
    runs = [(n, run) for n in range(len(PARTS)) for run in RUNS[n]]

    def run_copy(i, which):
        chip, row, rows = runs[i][1]
        src = fin.at[chip, row : row + rows, which * HD : (which + 1) * HD]
        dst = (pdk_o, pdv_o)[which].at[row : row + rows, cols(Z, HD)]
        return src, dst, chip

    def run_remote(i, which, d):
        src, dst, chip = run_copy(i, which)
        at = 2 * i + which
        return remote(src, dst, us.at[at, d - 1], ur.at[at, d - 1], (b, chip * 2 + K))

    def run_local(i, which):
        src, dst, chip = run_copy(i, which)
        return pltpu.make_async_copy(src, dst, us.at[2 * i + which, 3])

    def final(n):
        first, count = PARTS[n]
        for i in range(len(plane)):
            scattered[n, i].wait_recv()
        at, has = where_read(b)
        units = slice(first, first + count)
        total = acc[n][at, :, K] * has + from_c[n][b].astype(f32)
        total = total + acc_l[units, K] + ls_r[units].astype(f32)
        for i in range(len(plane)):
            total = total + from_p[n][i].astype(f32)
        total = total * scaled
        for u in range(count):
            chip, row = (first + u) // 2, (first + u) % 2 * UNIT
            pos = chip * 128 + K * 64 + row
            pos = pos + lax.broadcasted_iota(jnp.int32, (UNIT, 2 * HD), 0)
            fin[chip, row : row + UNIT, :] = jnp.where(pos < lens[b], total[u], 0.0).astype(bf16)
        for i, (part, (chip, _, _)) in enumerate(runs):
            if part == n:
                @pl.when(Z != chip)
                def _():
                    for which in (0, 1):
                        run_remote(i, which, (chip - Z + 4) % 4).start()

                @pl.when(Z == chip)
                def _():
                    for which in (0, 1):
                        run_local(i, which).start()

    def finals_done():
        for i, (_, (chip, _, _)) in enumerate(runs):
            @pl.when(Z != chip)
            def _():
                for which in (0, 1):
                    run_remote(i, which, (chip - Z + 4) % 4).wait_send()

            @pl.when(Z == chip)
            def _():
                for which in (0, 1):
                    run_local(i, which).wait()
                    for d in (1, 2, 3):
                        run_remote(i, which, d).wait_recv()

    def chunks(n, slots):
        count, slot_of = slots

        def one(i, _):
            cross(n, slot_of(i))
            return 0

        lax.fori_loop(0, count, one, 0)

    forward(0)
    z_out((4, 5), (2,))
    bfwd.wait_recv()
    self_chunk(0)
    forwarded(0)
    cross(0, 0)
    z_in((4, 5, 8), (1, 3))
    chunks(0, (2, lambda i: 1 + 2 * i))

    self_chunk(1)
    forward(1)
    plane_out(2)
    self_chunk(3)
    forwarded(1)
    cross(1, 0)
    z_in((4, 5, 8), (2,))
    z_out((6, 7), (1, 3, 2))
    cross(0, 2)
    to_core(0)
    cross(1, 1)
    to_plane(0)
    forward(2)
    plane_out(3)
    chunks(1, (2, lambda i: 3 - i))
    to_core(1)
    self_chunk(2)
    forwarded(2)
    cross(2, 0)
    to_plane(1)
    forward(3)
    chunks(2, (3, lambda i: i + 1))
    to_core(2)
    for c in own_p:
        c.wait()
    z_in((6, 7, 9), (1, 3, 2))
    forwarded(3)
    lax.fori_loop(0, 2, passage_chunk, 0)
    to_plane(2)
    for slot in (1, 3, 2):
        c = home(1, slot, pdqs.at[slot], pdq_o.at[:, cols(Z, WIDE)])
        c.start()
        back.append(c)
    own_out.append(local(pdqs.at[0], pdq_o.at[:, cols(Z, WIDE)]))
    ls_s[...] = acc_l[:, other].astype(bf16)
    moved_l = send(ls_s, ls_r, es.at[6], er.at[6], core)
    ss_s[...] = acc_s[:, other].astype(bf16)
    moved_s = send(ss_s, ss_r, es.at[4], er.at[4], core)

    def last_part(i, _):
        slot = jnp.where(i == 0, 2, 2 * i - 1)
        cross(3, slot)
        finish_dq(slot)
        dq_home(slot).start()
        return 0

    lax.fori_loop(0, 3, last_part, 0)
    moved_s.wait_recv()
    fin_s[...] = ((acc_s[:, K] + ss_r[...].astype(f32)) * scaled).astype(bf16)
    spread(2, fin_s, dk_o, dv_o)
    cross(3, 0)
    to_core(3)
    finish_dq(0)
    own_out.append(local(dqs.at[0], dq_o.at[:, cols(Z, WIDE)]))
    moved_l.wait_recv()
    final(0)
    to_plane(3)
    final(1)
    final(2)
    final(3)
    finals_done()
    for c in own_out:
        c.wait()
    for c in back:
        c.wait()
    for slot in (1, 2, 3):
        dq_home(slot).wait()
    for c in pending:
        c.wait_send()


def place(*refs):
    count = (len(refs) - 1) // 3
    ins, outs, held, sems = refs[:count], refs[count : 2 * count], refs[2 * count : -1], refs[-1]
    there = [pltpu.make_async_copy(ins[i], held[i], sems.at[0, i]) for i in range(count)]
    away = [pltpu.make_async_copy(held[i], outs[i], sems.at[1, i]) for i in range(count)]
    for c in there:
        c.start()
    for i in range(count):
        there[i].wait()
        away[i].start()
    for c in away:
        c.wait()


def shards(
    query_q, query_k, query_v, query_out, query_dout, query_lse, query_seg,
    passage_q, passage_k, passage_v, passage_out, passage_dout, passage_lse,
    passage_len, reads,
):
    hbm = pl.BlockSpec(memory_space=pl.ANY)
    vmem = pl.BlockSpec(memory_space=pltpu.VMEM)
    smem = pl.BlockSpec(memory_space=pltpu.SMEM)
    pair = 2 * HD
    V = pltpu.VMEM
    dma = pltpu.SemaphoreType.DMA
    wide = H * HD
    counts = [count for _, count in PARTS]
    parts = len(counts)
    stats = V((4, 16, 128), f32)
    scratch = [
        V((QROWS, wide), bf16), V((QROWS, wide), bf16), V((PROWS, wide), bf16), V((PROWS, wide), bf16),
        stats, stats, stats, stats,
        V((4, QROWS, WIDE), bf16), V((4, QROWS, WIDE), bf16),
        V((4, PROWS, WIDE), bf16), V((4, PROWS, WIDE), bf16),
        V((2, UNIT, 2 * KVH * HD), bf16), V((8, UNIT, pair), bf16),
        [V((PASSAGES, n, 2, UNIT, pair), bf16) for n in counts],
        V((4, 2, QROWS, pair), bf16), V((1024, 128), f32),
        V((4, HD, WIDE), f32),
        [V((READS, n, 2, UNIT, pair), f32) for n in counts],
        V((4, 2, QROWS, pair), f32), V((8, 2, UNIT, pair), f32),
        V((4, QROWS, WIDE), bf16), V((4, PROWS, WIDE), bf16),
        [V((PASSAGES, n, UNIT, pair), bf16) for n in counts],
        [V((PASSAGES, n, UNIT, pair), bf16) for n in counts],
        [V((PASSAGES, n, UNIT, pair), bf16) for n in counts],
        [V((PASSAGES - 1, n, UNIT, pair), bf16) for n in counts],
        V((8, UNIT, pair), bf16), V((8, UNIT, pair), bf16),
        V((4, QROWS, pair), bf16), V((4, QROWS, pair), bf16),
        V((4, PROWS, pair), bf16), V((4, QROWS, pair), bf16),
        dma((10, 3)), dma((10, 3)), dma((parts, 15)), dma((parts, 15)),
        dma((parts, 4)), dma((parts, 4)),
        dma((7,)), dma((7,)), dma((parts, 15)), dma((parts, 15)), dma((4, 3)), dma((4, 3)),
        dma((12, 4)), dma((12, 3)), dma((24,)),
    ]
    shape = jax.ShapeDtypeStruct
    results = (
        shape((QROWS, wide), bf16), shape((QROWS, KVH * HD), bf16), shape((QROWS, KVH * HD), bf16),
        shape((PROWS, wide), bf16), shape((PROWS, KVH * HD), bf16), shape((PROWS, KVH * HD), bf16),
    )
    found = pl.pallas_call(
        body,
        out_shape=results,
        in_specs=[smem, smem, hbm, hbm, hbm, hbm, hbm, vmem, vmem, hbm, hbm, hbm, hbm, hbm, vmem],
        out_specs=(hbm,) * 6,
        scratch_shapes=scratch,
        compiler_params=pltpu.CompilerParams(
            collective_id=0, has_side_effects=True, vmem_limit_bytes=60 * 2**20
        ),
    )(
        reads.T, passage_len,
        query_q, query_k, query_v, query_out, query_dout, query_lse, query_seg,
        passage_q, passage_k, passage_v, passage_out, passage_dout, passage_lse,
    )
    return pl.pallas_call(
        place,
        out_shape=results,
        in_specs=[hbm] * 6,
        out_specs=(hbm,) * 6,
        scratch_shapes=[V(x.shape, bf16) for x in results] + [dma((2, 6))],
    )(*found)


def solution(mesh):
    rows = P(("pass", "query"), None)
    along = P(None, ("pass", "query"))
    return jax.shard_map(
        shards,
        mesh=mesh,
        in_specs=(
            rows, rows, rows, rows, rows, along, P("pass", None),
            rows, rows, rows, rows, rows, along, P(), P(),
        ),
        out_specs=(rows,) * 6,
        check_vma=False,
    )
```
